32 devices in a mesh: occ: 4 (over y, x), vir: 8 (over z, core).
Axes of the slice: x: 2, y: 2, z: 4, core: 2. Of those that a mesh axis runs over, the one named last changes fastest.
Arguments:
- factors: bfloat16 [256, 1024, 2048], P(None, 'vir', 'occ'), may hold values from -0.125 to 0.125
- e_occ: float32 [256], replicated, may hold values from -2 to -0.3
- e_vir: float32 [1024], replicated, may hold values from 0.1 to 3
- i_sub: int32 [3], replicated, may hold values from 0 to 3
- j_row: int32 [3], replicated, may hold values from 0 to 255
Outputs:
- density: float32 [256, 1024, 2048], P(None, 'vir', 'occ')
The draws below stay inside these ranges and needn't reach their ends.
All inputs are finite; a program needn't handle non-finite values.
Results may differ from the reference program's by a relative error of at most 0.0022.
Values may be sent and summed in bfloat16 or wider, within the bound.
No kernel may reach another device: no remote copies, remote signals or barrier semaphores. Data moves between devices by JAX's collectives and lax.ppermute only.
A program may use at most 320 MiB of HBM per device.

```python
import jax
import jax.numpy as jnp
from jax import lax

NOCC = 256
NVIR = 1024
NAUX = 2048
IBK = 16
STEPS = 3
SUBS = 4
N_OCC = 4


def steps_of(key, shape, split, smallest, high):
    factor_of = 1.0
    for dim, shards_of in split:
        steps = jax.random.uniform(jax.random.fold_in(jax.random.fold_in(key, 6), dim), (shards_of,), jnp.float32, smallest / len(split), high / len(split))
        factor_of = factor_of * jnp.repeat(jnp.exp(steps), shape[dim] // shards_of).reshape((-1,) + (1,) * (len(shape) - 1 - dim))
    return factor_of


def bell_draw(stream_key, dims, scale, reach, shards=(), dtype=jnp.bfloat16):
    array = scale * jax.random.normal(stream_key, dims, jnp.float32)
    if shards:
        array = array * steps_of(stream_key, dims, shards, -0.22, 0.18)
    return jnp.clip(array, -reach, reach).astype(dtype)


def setup_inputs(seed: int = 0) -> dict:
    streams_of = jax.random.split(jax.random.key(seed), 6)
    return {
        "factors": bell_draw(streams_of[0], (NOCC, NVIR, NAUX), NAUX ** -0.5, 0.125, ((1, 8), (2, 4))),
        "e_occ": jnp.clip(jax.random.uniform(streams_of[1], (NOCC,), jnp.float32, -2.0, -0.3), -2.0, -0.3),
        "e_vir": jnp.clip(jax.random.uniform(streams_of[2], (NVIR,), jnp.float32, 0.1, 3.0), 0.1, 3.0),
        "i_sub": jax.random.randint(streams_of[3], (STEPS,), 0, SUBS).astype(jnp.int32),
        "j_row": jax.random.randint(streams_of[4], (STEPS,), 0, NOCC).astype(jnp.int32),
    }


def reference(factors, e_occ, e_vir, i_sub, j_row):
    owned = NOCC // N_OCC
    density = jnp.zeros((NOCC, NVIR, NAUX), jnp.float32)
    for step_index in range(STEPS):
        j_index = j_row[step_index]
        pair_slab = lax.dynamic_index_in_dim(factors, j_index, 0, keepdims=False).astype(jnp.float32)
        energy_pair = e_occ[j_index]
        offset = i_sub[step_index] * IBK

        def owner_step(owner, density):
            first_row = (owner * owned + offset).astype(jnp.int32)
            row_block = lax.dynamic_slice_in_dim(factors, first_row, IBK, 0).astype(jnp.float32)
            energy_rows = lax.dynamic_slice_in_dim(e_occ, first_row, IBK, 0)
            integrals = jnp.einsum("iap,bp->iab", row_block, pair_slab)
            denominator = e_vir[None, :, None] + e_vir[None, None, :] - energy_rows[:, None, None] - energy_pair
            amplitude = (-integrals / denominator).astype(jnp.bfloat16)
            contribution = jnp.einsum("iab,bp->iap", amplitude.astype(jnp.float32), pair_slab)
            previous = lax.dynamic_slice_in_dim(density, first_row, IBK, 0)
            return lax.dynamic_update_slice_in_dim(density, previous + contribution, first_row, 0)

        density = lax.fori_loop(0, N_OCC, owner_step, density)
    return density
```

```python
import functools

import jax
import jax.numpy as jnp
from jax import lax
from jax.experimental import pallas as pl
from jax.experimental.pallas import tpu as pltpu
from jax.sharding import PartitionSpec as P

IBK = 16
CODE_MAX = 32767.0
SCALE_MIN = 1e-33


def exchange(piece, partner):
    size = lax.axis_size("occ")
    return lax.ppermute(piece, "occ", [(r, r ^ partner) for r in range(size)])


def pair_kernel(n_steps, n_occ, first_ref, shift_ref, own_ref, *refs):
    row_refs = (own_ref,) + refs[: n_occ - 1]
    refs = refs[n_occ - 1 :]
    e_own_ref, e_vir_ref = refs[:2]
    slab_refs = refs[2 : 2 + n_steps]
    refs = refs[2 + n_steps :]
    own_out = refs[0]
    code_refs = refs[1:n_occ]
    scale_refs = refs[n_occ : 2 * n_occ - 1]
    amp_ref = refs[2 * n_occ - 1]
    ib, vir_own, aux_own = own_ref.shape
    rows = ib * vir_own
    block = pl.program_id(0)
    for n in range(n_steps):
        integrals = None
        for m in range(n_occ):
            term = lax.dot_general(
                row_refs[m][...].reshape(rows, aux_own),
                slab_refs[n][:, m * aux_own : (m + 1) * aux_own],
                (((1,), (1,)), ((), ())),
                preferred_element_type=jnp.float32,
            )
            integrals = term if integrals is None else integrals + term
        for k in range(ib):
            part = integrals[k * vir_own : (k + 1) * vir_own]
            denominator = e_own_ref[...] + (e_vir_ref[...] - shift_ref[n, block * ib + k])
            amp_ref[n, k * vir_own : (k + 1) * vir_own, :] = (-part / denominator).astype(jnp.bfloat16)
    for m in range(n_occ):
        density = None
        for n in range(n_steps):
            term = jnp.dot(
                amp_ref[n],
                slab_refs[n][:, m * aux_own : (m + 1) * aux_own],
                preferred_element_type=jnp.float32,
            )
            density = term if density is None else density + term
        density = density.reshape(ib, vir_own, aux_own)
        if m == 0:
            own_out[...] = density
        else:
            largest = jnp.maximum(jnp.max(jnp.abs(density), axis=2, keepdims=True), SCALE_MIN)
            codes = jnp.round(density * (CODE_MAX / largest))
            code_refs[m - 1][...] = codes.astype(jnp.int32).astype(jnp.int16)
            scale_refs[m - 1][...] = (largest * (1.0 / CODE_MAX)).reshape(ib, 1, vir_own)


def pair_block(factors, first_row, received, slabs, shift, e_own, e_vir):
    n_steps, n_occ = len(slabs), len(received) + 1
    _, vir_own, aux_own = factors.shape
    vir_total, aux_total = slabs[0].shape
    ib = max(1, min(IBK, 512 // vir_own))
    rows = ib * vir_own
    whole = pl.BlockSpec(memory_space=pltpu.VMEM)
    piece = pl.BlockSpec((ib, vir_own, aux_own), lambda i, first: (i, 0, 0))
    scale = pl.BlockSpec((ib, 1, vir_own), lambda i, first: (i, 0, 0))
    flops = 4 * IBK * vir_own * vir_total * aux_total * n_steps
    outs = pl.pallas_call(
        functools.partial(pair_kernel, n_steps, n_occ),
        grid_spec=pltpu.PrefetchScalarGridSpec(
            num_scalar_prefetch=1,
            grid=(IBK // ib,),
            in_specs=[
                pl.BlockSpec(memory_space=pltpu.SMEM),
                pl.BlockSpec((ib, vir_own, aux_own), lambda i, first: (first[0] + i, 0, 0)),
            ]
            + [piece] * (n_occ - 1)
            + [whole] * (2 + n_steps),
            out_specs=[piece] * n_occ + [scale] * (n_occ - 1),
            scratch_shapes=[pltpu.VMEM((n_steps, rows, vir_total), jnp.bfloat16)],
        ),
        out_shape=[jax.ShapeDtypeStruct((IBK, vir_own, aux_own), jnp.float32)]
        + [jax.ShapeDtypeStruct((IBK, vir_own, aux_own), jnp.int16)] * (n_occ - 1)
        + [jax.ShapeDtypeStruct((IBK, 1, vir_own), jnp.float32)] * (n_occ - 1),
        compiler_params=pltpu.CompilerParams(vmem_limit_bytes=48 * 2**20),
        cost_estimate=pl.CostEstimate(flops=flops, bytes_accessed=16 * 2**20, transcendentals=0),
    )(
        jnp.reshape(first_row // ib, (1,)).astype(jnp.int32),
        shift,
        factors,
        *received,
        e_own[:, None],
        e_vir[None, :],
        *slabs,
    )
    return outs[0], outs[1:n_occ], outs[n_occ:]


def planned(sizes, factors, e_occ, e_vir, subs, rows_j):
    total, vir_own, aux_own = factors.shape
    n_occ = lax.axis_size("occ")
    owned = total // n_occ
    rank = lax.axis_index("occ")
    steps = subs.shape[0]
    e_own = lax.dynamic_slice_in_dim(e_vir, lax.axis_index("vir") * vir_own, vir_own, 0)

    def rows_of(owner, offset):
        return lax.dynamic_slice_in_dim(factors, owner * owned + offset, IBK, 0)

    pair_own = jnp.stack([lax.dynamic_index_in_dim(factors, rows_j[s], 0, keepdims=False) for s in range(steps)])
    pair_rows = jnp.concatenate([pair_own] + [exchange(pair_own, m) for m in range(1, n_occ)], axis=2)
    slabs = [lax.all_gather(pair_rows[s], "vir", axis=0, tiled=True) for s in range(steps)]

    starts = [sum(sizes[:u]) for u in range(len(sizes))]
    offsets = [subs[s] * IBK for s in starts]
    received = [[exchange(rows_of(rank ^ m, offset), m) for m in range(1, n_occ)] for offset in offsets]
    density = jnp.zeros(factors.shape, jnp.float32)
    for u, size in enumerate(sizes):
        first = rank * owned + offsets[u]
        e_rows = lax.dynamic_slice_in_dim(e_occ, first, IBK, 0)
        members = range(starts[u], starts[u] + size)
        shift = jnp.stack([e_rows + e_occ[rows_j[s]] for s in members])
        own, codes, scales = pair_block(
            factors, first, received[u], [slabs[s] for s in members], shift, e_own, e_vir
        )
        density = lax.dynamic_update_slice_in_dim(density, own, first, 0)
        for m in range(1, n_occ):
            scale = exchange(scales[m - 1], m)
            code = exchange(codes[m - 1], m)
            part = code.astype(jnp.float32) * scale.reshape(IBK, vir_own, 1)
            density = lax.dynamic_update_slice_in_dim(density, part, (rank ^ m) * owned + offsets[u], 0)
    return density


def partitions(total, largest):
    if total == 0:
        return [()]
    return [rest + (p,) for p in range(min(total, largest), 0, -1) for rest in partitions(total - p, p)]


def shards(factors, e_occ, e_vir, i_sub, j_row):
    steps = i_sub.shape[0]
    subs_held = factors.shape[0] // lax.axis_size("occ") // IBK
    shared = jnp.sum(i_sub[:, None] == i_sub[None, :], axis=1).astype(jnp.int32)
    order = jnp.argsort((shared * (subs_held + 1) + i_sub) * steps + jnp.arange(steps, dtype=jnp.int32))
    sizes_list = [p for p in partitions(steps, steps) if len(p) <= subs_held]
    sizes_of = jnp.array([sum(([p] * p for p in sizes), []) for sizes in sizes_list], jnp.int32)
    branch = jnp.argmax(jnp.all(sizes_of == shared[order][None, :], axis=1)).astype(jnp.int32)
    return lax.switch(
        branch,
        [functools.partial(planned, sizes) for sizes in sizes_list],
        factors,
        e_occ,
        e_vir,
        i_sub[order],
        j_row[order],
    )


def solution(mesh):
    placed = (P(None, "vir", "occ"), P(), P(), P(), P())
    return jax.shard_map(
        shards, mesh=mesh, in_specs=placed, out_specs=P(None, "vir", "occ"), check_vma=False
    )
```

```python
import functools

import jax
import jax.numpy as jnp
from jax import lax
from jax.experimental import pallas as pl
from jax.experimental.pallas import tpu as pltpu
from jax.sharding import PartitionSpec as P

IBK = 16
CODE_MAX = 32767.0
LARGEST_MIN = 1e-33
TAIL = 16


def exchange(piece, partner):
    size = lax.axis_size("occ")
    return lax.ppermute(piece, "occ", [(r, r ^ partner) for r in range(size)])


def after(values, *earlier):
    return lax.optimization_barrier((values, earlier))[0]


def swapped(pieces):
    return {m: exchange(piece, m) for m, piece in pieces.items()}


def rounds_of(n_occ, turn):
    masks = range(1, n_occ)
    near = tuple(m for m in masks if m & (m - 1) == 0)
    rounds = [near] + [(m,) for m in masks if m not in near]
    return rounds if turn % 2 else rounds[::-1]


def pair_kernel(n_steps, n_occ, entry, skip, row_entries, plan_ref, e_occ_ref, own_ref, *refs):
    row_refs = (own_ref,) + refs[: n_occ - 1]
    refs = refs[n_occ - 1 :]
    e_own_ref, e_vir_ref = refs[:2]
    slab_refs = refs[2 : 2 + n_steps]
    own_out = refs[3 + n_steps]
    code_refs = refs[4 + n_steps : 3 + n_steps + n_occ]
    amp_ref, power_ref = refs[3 + n_steps + n_occ :]
    ib, vir_own, aux_own = own_ref.shape
    rows = ib * vir_own
    vir_total = e_vir_ref.shape[1]
    block = pl.program_id(0)
    wide = min(256, vir_total)

    for n in range(n_steps):

        def integrals_of(c, carry, n=n):
            at = pl.ds(pl.multiple_of(c * wide, wide), wide)
            integrals = None
            for m in range(n_occ):
                term = lax.dot_general(
                    row_refs[m][...].reshape(rows, aux_own),
                    slab_refs[n][at, m * aux_own : (m + 1) * aux_own],
                    (((1,), (1,)), ((), ())),
                    preferred_element_type=jnp.float32,
                )
                integrals = term if integrals is None else integrals + term
            e_pair = e_occ_ref[plan_ref[row_entries[n]]]
            for k in range(ib):
                shift = e_occ_ref[plan_ref[entry] + skip + block * ib + k] + e_pair
                part = integrals[k * vir_own : (k + 1) * vir_own]
                denominator = e_own_ref[...] + (e_vir_ref[:, at] - shift)
                amp_ref[n, k * vir_own : (k + 1) * vir_own, at] = (-part / denominator).astype(jnp.bfloat16)
            return carry

        lax.fori_loop(0, vir_total // wide, integrals_of, 0)

    tall = min(256, rows)
    held = tall // vir_own

    def density_of(r, carry):
        at = pl.ds(pl.multiple_of(r * tall, tall), tall)
        for m in range(n_occ):
            density = None
            for n in range(n_steps):
                term = jnp.dot(
                    amp_ref[n, at, :],
                    slab_refs[n][:, m * aux_own : (m + 1) * aux_own],
                    preferred_element_type=jnp.float32,
                )
                density = term if density is None else density + term
            if m == 0:
                own_out[pl.ds(r * held, held)] = density.reshape(held, vir_own, aux_own)
            else:
                largest = jnp.maximum(jnp.max(jnp.abs(density), axis=1, keepdims=True), LARGEST_MIN)
                power = jnp.floor(jnp.log2(CODE_MAX / largest))
                codes = jnp.clip(jnp.round(density * jnp.exp2(power)), -CODE_MAX, CODE_MAX)
                at_all = pl.ds(pl.multiple_of(block * rows + r * tall, tall), tall)
                code_refs[m - 1][at_all, :] = codes.astype(jnp.int32).astype(jnp.int16)
                power_ref[m - 1, pl.ds(block * ib + r * held, held), :] = power.reshape(held, vir_own)
        return carry

    lax.fori_loop(0, rows // tall, density_of, 0)

    @pl.when(block == pl.num_programs(0) - 1)
    def _():
        for m in range(1, n_occ):
            last = code_refs[m - 1].shape[0] - TAIL
            powers = power_ref[m - 1].astype(jnp.int32).astype(jnp.int16)
            code_refs[m - 1][last:, :] = jnp.zeros((TAIL, aux_own), jnp.int16)
            code_refs[m - 1][last:, :vir_own] = powers


def blocks_of(count, vir_own):
    return max(1, min(count, 512 // vir_own))


def picked(factors, plan, entries, count):
    _, vir_own, aux_own = factors.shape
    ib = min(4, count)

    def body(plan_ref, *refs):
        half = len(refs) // 2
        for source, target in zip(refs[:half], refs[half:]):
            target[...] = source[...]

    def source_of(entry, skip):
        return pl.BlockSpec((ib, vir_own, aux_own), lambda i, plan: (plan[entry] // ib + skip // ib + i, 0, 0))

    return pl.pallas_call(
        body,
        grid_spec=pltpu.PrefetchScalarGridSpec(
            num_scalar_prefetch=1,
            grid=(count // ib,),
            in_specs=[source_of(*entry) for entry in entries],
            out_specs=[pl.BlockSpec((ib, vir_own, aux_own), lambda i, plan: (i, 0, 0))] * len(entries),
        ),
        out_shape=[jax.ShapeDtypeStruct((count, vir_own, aux_own), factors.dtype)] * len(entries),
        compiler_params=pltpu.CompilerParams(vmem_limit_bytes=48 * 2**20),
        cost_estimate=pl.CostEstimate(
            flops=0, bytes_accessed=4 * len(entries) * count * vir_own * aux_own, transcendentals=0
        ),
    )(plan, *([factors] * len(entries)))


def pair_block(density, factors, plan, e_occ, entry, skip, row_entries, received, slabs, members, e_own, e_vir):
    n_steps, n_occ = len(members), len(received) + 1
    count, vir_own, aux_own = received[0].shape
    vir_total, aux_total = slabs.shape[0], n_occ * aux_own
    ib = blocks_of(count, vir_own)
    rows = ib * vir_own
    whole = pl.BlockSpec(memory_space=pltpu.VMEM)
    piece = pl.BlockSpec((ib, vir_own, aux_own), lambda i, plan: (i, 0, 0))
    own = pl.BlockSpec((ib, vir_own, aux_own), lambda i, plan: (plan[entry] // ib + skip // ib + i, 0, 0))
    coded = (count * vir_own + TAIL, aux_own)
    flops = 4 * count * vir_own * vir_total * aux_total * n_steps
    outs = pl.pallas_call(
        functools.partial(pair_kernel, n_steps, n_occ, entry, skip, row_entries),
        grid_spec=pltpu.PrefetchScalarGridSpec(
            num_scalar_prefetch=1,
            grid=(count // ib,),
            in_specs=[pl.BlockSpec(memory_space=pltpu.SMEM), own]
            + [piece] * (n_occ - 1)
            + [whole] * 2
            + [pl.BlockSpec((vir_total, aux_total), lambda i, plan, s=s: (0, s)) for s in members]
            + [pl.BlockSpec(memory_space=pl.ANY)],
            out_specs=[own] + [pl.BlockSpec(coded, lambda i, plan: (0, 0))] * (n_occ - 1),
            scratch_shapes=[
                pltpu.VMEM((n_steps, rows, vir_total), jnp.bfloat16),
                pltpu.VMEM((n_occ - 1, TAIL, vir_own), jnp.float32),
            ],
        ),
        out_shape=[jax.ShapeDtypeStruct(density.shape, jnp.float32)]
        + [jax.ShapeDtypeStruct(coded, jnp.int16)] * (n_occ - 1),
        input_output_aliases={n_occ + n_steps + 4: 0},
        compiler_params=pltpu.CompilerParams(vmem_limit_bytes=48 * 2**20),
        cost_estimate=pl.CostEstimate(flops=flops, bytes_accessed=16 * 2**20, transcendentals=0),
    )(plan, e_occ, factors, *received, e_own[:, None], e_vir[None, :], *([slabs] * n_steps), density)
    return outs[0], outs[1:]


def decoded(density, plan, entry, skip, codes, count):
    _, vir_own, aux_own = density.shape
    ib = blocks_of(count, vir_own)

    def body(plan_ref, code_ref, power_ref, density_ref, out_ref):
        block = pl.program_id(0)
        powers = power_ref[...].astype(jnp.float32)[:, :vir_own]
        for k in range(ib):
            at = jax.lax.broadcasted_iota(jnp.int32, powers.shape, 0) == block * ib + k
            power = jnp.sum(jnp.where(at, powers, 0.0), axis=0, keepdims=True)
            scale = jnp.exp2(-jnp.broadcast_to(power, (8, vir_own)).T[:, :1])
            part = code_ref[k * vir_own : (k + 1) * vir_own, :].astype(jnp.float32)
            out_ref[k] = part * scale

    return pl.pallas_call(
        body,
        grid_spec=pltpu.PrefetchScalarGridSpec(
            num_scalar_prefetch=1,
            grid=(count // ib,),
            in_specs=[
                pl.BlockSpec((ib * vir_own, aux_own), lambda i, plan: (i, 0)),
                pl.BlockSpec((TAIL, aux_own), lambda i, plan: (count * vir_own // TAIL, 0)),
                pl.BlockSpec(memory_space=pl.ANY),
            ],
            out_specs=pl.BlockSpec(
                (ib, vir_own, aux_own), lambda i, plan: (plan[entry] // ib + skip // ib + i, 0, 0)
            ),
        ),
        out_shape=jax.ShapeDtypeStruct(density.shape, jnp.float32),
        input_output_aliases={3: 0},
        compiler_params=pltpu.CompilerParams(vmem_limit_bytes=24 * 2**20),
        cost_estimate=pl.CostEstimate(
            flops=0, bytes_accessed=6 * count * vir_own * aux_own, transcendentals=0
        ),
    )(plan, codes, codes, density)


def planned(sizes, factors, e_occ, e_vir, e_own, plan):
    n_occ = lax.axis_size("occ")
    steps = sum(sizes)

    def entry_of(step, partner):
        return step * n_occ + partner

    def row_entry_of(step):
        return steps * n_occ + step

    cuts = 2 if len(sizes) == 1 else 1
    count = IBK // cuts
    starts = [sum(sizes[:u]) for u in range(len(sizes))]
    items = [(u, cut * count) for u in range(len(sizes)) for cut in range(cuts)]
    pair_own = picked(factors, plan, [(row_entry_of(s), 0) for s in range(steps)], 1)
    pair_got = swapped({m: jnp.concatenate(pair_own, axis=0) for m in range(1, n_occ)})
    density = None
    received = []
    for turn, (u, skip) in enumerate(items):
        at = plan if turn == 0 else after(plan, density)
        got = {}
        for partners in rounds_of(n_occ, turn):
            entries = [(entry_of(starts[u], m), skip) for m in partners]
            pieces = dict(zip(partners, picked(factors, at, entries, count)))
            if turn == 0:
                pair_got = after(pair_got, pieces)
            got.update(swapped(pieces))
        received.append([got[m] for m in range(1, n_occ)])
        if turn == 0:
            density = jnp.full(factors.shape, after(jnp.float32(0.0), pair_got[1]), jnp.float32)

    pair_rows = jnp.concatenate(
        [part for s in range(steps) for part in [pair_own[s][0]] + [pair_got[m][s] for m in range(1, n_occ)]],
        axis=1,
    )
    slabs = lax.all_gather(pair_rows, "vir", axis=0, tiled=True)

    coded = []
    for (u, skip), pieces in zip(items, received):
        members = range(starts[u], starts[u] + sizes[u])
        density, codes = pair_block(
            density,
            factors,
            plan,
            e_occ,
            entry_of(starts[u], 0),
            skip,
            [row_entry_of(s) for s in members],
            pieces,
            slabs,
            members,
            e_own,
            e_vir,
        )
        coded.append(codes)

    for turn, ((u, skip), codes) in enumerate(zip(items, coded), len(items)):
        for partners in rounds_of(n_occ, turn):
            got = swapped({m: codes[m - 1] for m in partners})
            for m in partners:
                density = decoded(density, plan, entry_of(starts[u], m), skip, got[m], count)
    return density


def partitions(total, largest):
    if total == 0:
        return [()]
    return [rest + (p,) for p in range(min(total, largest), 0, -1) for rest in partitions(total - p, p)]


def plan_kernel(sizes_list, owned, n_occ, sub_ref, row_ref, plan_ref, branch_ref):
    steps = sub_ref.shape[0]
    subs = [sub_ref[s] for s in range(steps)]

    def total(terms):
        return functools.reduce(lambda a, b: a + b, terms)

    def chosen(holds, value=1):
        return jnp.where(holds, jnp.int32(value), jnp.int32(0))

    shared = [total([chosen(subs[s] == subs[t]) for t in range(steps)]) for s in range(steps)]
    keys = [(shared[s] * (owned // IBK) + subs[s]) * steps + s for s in range(steps)]
    places = [total([chosen(keys[t] < keys[s]) for t in range(steps)]) for s in range(steps)]
    me = lax.axis_index("occ")
    found = []
    for p in range(steps):
        sub = total([chosen(places[s] == p, subs[s]) for s in range(steps)])
        plan_ref[steps * n_occ + p] = total([chosen(places[s] == p, row_ref[s]) for s in range(steps)])
        found.append(total([chosen(places[s] == p, shared[s]) for s in range(steps)]))
        for m in range(n_occ):
            plan_ref[p * n_occ + m] = (me ^ m) * owned + sub * IBK
    branch = jnp.int32(0)
    for b, sizes in enumerate(sizes_list):
        wanted = sum(([p] * p for p in sizes), [])
        missed = total([chosen(have != want) for have, want in zip(found, wanted)])
        branch = jnp.where(missed == 0, jnp.int32(b), branch)
    branch_ref[0] = branch


def shards(factors, e_occ, e_vir, i_sub, j_row):
    vir_own = factors.shape[1]
    n_occ = lax.axis_size("occ")
    owned = factors.shape[0] // n_occ
    steps = i_sub.shape[0]
    sizes_list = [p for p in partitions(steps, steps) if len(p) <= owned // IBK]
    sizes_list.sort(key=lambda sizes: abs(len(sizes) - 2))
    scalars = pl.BlockSpec(memory_space=pltpu.SMEM)
    plan, branch = pl.pallas_call(
        functools.partial(plan_kernel, sizes_list, owned, n_occ),
        in_specs=[scalars, scalars],
        out_specs=[scalars, scalars],
        out_shape=[
            jax.ShapeDtypeStruct((steps * (n_occ + 1),), jnp.int32),
            jax.ShapeDtypeStruct((1,), jnp.int32),
        ],
    )(i_sub, j_row)
    e_own = lax.dynamic_slice_in_dim(e_vir, lax.axis_index("vir") * vir_own, vir_own, 0)
    return lax.switch(
        branch[0],
        [functools.partial(planned, sizes) for sizes in sizes_list],
        factors,
        e_occ,
        e_vir,
        e_own,
        plan,
    )


def solution(mesh):
    placed = (P(None, "vir", "occ"), P(), P(), P(), P())
    return jax.shard_map(
        shards, mesh=mesh, in_specs=placed, out_specs=P(None, "vir", "occ"), check_vma=False
    )
```

```python
import functools

import jax
import jax.numpy as jnp
from jax import lax
from jax.experimental import pallas as pl
from jax.experimental.pallas import tpu as pltpu
from jax.sharding import PartitionSpec as P

IBK = 16
CODE_MAX = 32767.0
LARGEST_MIN = 1e-33
TAIL = 16


def exchange(piece, partner):
    size = lax.axis_size("occ")
    return lax.ppermute(piece, "occ", [(r, r ^ partner) for r in range(size)])


def after(values, *earlier):
    return lax.optimization_barrier((values, earlier))[0]


def swapped(pieces):
    return {m: exchange(piece, m) for m, piece in pieces.items()}


def rounds_of(n_occ, turn):
    masks = range(1, n_occ)
    near = tuple(m for m in masks if m & (m - 1) == 0)
    rounds = [near] + [(m,) for m in masks if m not in near]
    return rounds if turn % 2 else rounds[::-1]


def pair_kernel(n_steps, n_occ, entry, skip, row_entries, plan_ref, e_occ_ref, own_ref, *refs):
    row_refs = (own_ref,) + refs[: n_occ - 1]
    refs = refs[n_occ - 1 :]
    e_own_ref, e_vir_ref = refs[:2]
    slab_refs = refs[2 : 2 + n_steps]
    own_out = refs[3 + n_steps]
    code_refs = refs[4 + n_steps : 3 + n_steps + n_occ]
    amp_ref, power_ref = refs[3 + n_steps + n_occ :]
    ib, vir_own, aux_own = own_ref.shape
    rows = ib * vir_own
    vir_total = e_vir_ref.shape[1]
    block = pl.program_id(0)
    wide = min(256, vir_total)

    for n in range(n_steps):

        def integrals_of(c, carry, n=n):
            at = pl.ds(pl.multiple_of(c * wide, wide), wide)
            integrals = None
            for m in range(n_occ):
                term = lax.dot_general(
                    row_refs[m][...].reshape(rows, aux_own),
                    slab_refs[n][at, m * aux_own : (m + 1) * aux_own],
                    (((1,), (1,)), ((), ())),
                    preferred_element_type=jnp.float32,
                )
                integrals = term if integrals is None else integrals + term
            e_pair = e_occ_ref[plan_ref[row_entries[n]]]
            for k in range(ib):
                shift = e_occ_ref[plan_ref[entry] + skip + block * ib + k] + e_pair
                part = integrals[k * vir_own : (k + 1) * vir_own]
                denominator = e_own_ref[...] + (e_vir_ref[:, at] - shift)
                amp_ref[n, k * vir_own : (k + 1) * vir_own, at] = (-part / denominator).astype(jnp.bfloat16)
            return carry

        lax.fori_loop(0, vir_total // wide, integrals_of, 0)

    tall = min(256, rows)
    held = tall // vir_own

    def density_of(r, carry):
        at = pl.ds(pl.multiple_of(r * tall, tall), tall)
        for m in range(n_occ):
            density = None
            for n in range(n_steps):
                term = jnp.dot(
                    amp_ref[n, at, :],
                    slab_refs[n][:, m * aux_own : (m + 1) * aux_own],
                    preferred_element_type=jnp.float32,
                )
                density = term if density is None else density + term
            if m == 0:
                own_out[pl.ds(r * held, held)] = density.reshape(held, vir_own, aux_own)
            else:
                largest = jnp.maximum(jnp.max(jnp.abs(density), axis=1, keepdims=True), LARGEST_MIN)
                power = jnp.floor(jnp.log2(CODE_MAX / largest))
                codes = jnp.clip(jnp.round(density * jnp.exp2(power)), -CODE_MAX, CODE_MAX)
                at_all = pl.ds(pl.multiple_of(block * rows + r * tall, tall), tall)
                code_refs[m - 1][at_all, :] = codes.astype(jnp.int32).astype(jnp.int16)
                power_ref[m - 1, pl.ds(block * ib + r * held, held), :] = power.reshape(held, vir_own)
        return carry

    lax.fori_loop(0, rows // tall, density_of, 0)

    @pl.when(block == pl.num_programs(0) - 1)
    def _():
        for m in range(1, n_occ):
            last = code_refs[m - 1].shape[0] - TAIL
            powers = power_ref[m - 1].astype(jnp.int32).astype(jnp.int16)
            code_refs[m - 1][last:, :] = jnp.zeros((TAIL, aux_own), jnp.int16)
            code_refs[m - 1][last:, :vir_own] = powers


def blocks_of(count, vir_own):
    return max(1, min(count, 512 // vir_own))


def picked(factors, plan, entries, count):
    _, vir_own, aux_own = factors.shape
    ib = min(4, count)

    def body(plan_ref, *refs):
        half = len(refs) // 2
        for source, target in zip(refs[:half], refs[half:]):
            target[...] = source[...]

    def source_of(entry, skip):
        return pl.BlockSpec((ib, vir_own, aux_own), lambda i, plan: (plan[entry] // ib + skip // ib + i, 0, 0))

    return pl.pallas_call(
        body,
        grid_spec=pltpu.PrefetchScalarGridSpec(
            num_scalar_prefetch=1,
            grid=(count // ib,),
            in_specs=[source_of(*entry) for entry in entries],
            out_specs=[pl.BlockSpec((ib, vir_own, aux_own), lambda i, plan: (i, 0, 0))] * len(entries),
        ),
        out_shape=[jax.ShapeDtypeStruct((count, vir_own, aux_own), factors.dtype)] * len(entries),
        compiler_params=pltpu.CompilerParams(vmem_limit_bytes=48 * 2**20),
        cost_estimate=pl.CostEstimate(
            flops=0, bytes_accessed=4 * len(entries) * count * vir_own * aux_own, transcendentals=0
        ),
    )(plan, *([factors] * len(entries)))


def pair_block(density, factors, plan, e_occ, entry, skip, row_entries, received, slabs, members, e_own, e_vir):
    n_steps, n_occ = len(members), len(received) + 1
    count, vir_own, aux_own = received[0].shape
    vir_total, aux_total = slabs.shape[0], n_occ * aux_own
    ib = blocks_of(count, vir_own)
    rows = ib * vir_own
    whole = pl.BlockSpec(memory_space=pltpu.VMEM)
    piece = pl.BlockSpec((ib, vir_own, aux_own), lambda i, plan: (i, 0, 0))
    own = pl.BlockSpec((ib, vir_own, aux_own), lambda i, plan: (plan[entry] // ib + skip // ib + i, 0, 0))
    coded = (count * vir_own + TAIL, aux_own)
    flops = 4 * count * vir_own * vir_total * aux_total * n_steps
    outs = pl.pallas_call(
        functools.partial(pair_kernel, n_steps, n_occ, entry, skip, row_entries),
        grid_spec=pltpu.PrefetchScalarGridSpec(
            num_scalar_prefetch=1,
            grid=(count // ib,),
            in_specs=[pl.BlockSpec(memory_space=pltpu.SMEM), own]
            + [piece] * (n_occ - 1)
            + [whole] * 2
            + [pl.BlockSpec((vir_total, aux_total), lambda i, plan, s=s: (0, s)) for s in members]
            + [pl.BlockSpec(memory_space=pl.ANY)],
            out_specs=[own] + [pl.BlockSpec(coded, lambda i, plan: (0, 0))] * (n_occ - 1),
            scratch_shapes=[
                pltpu.VMEM((n_steps, rows, vir_total), jnp.bfloat16),
                pltpu.VMEM((n_occ - 1, TAIL, vir_own), jnp.float32),
            ],
        ),
        out_shape=[jax.ShapeDtypeStruct(density.shape, jnp.float32)]
        + [jax.ShapeDtypeStruct(coded, jnp.int16)] * (n_occ - 1),
        input_output_aliases={n_occ + n_steps + 4: 0},
        compiler_params=pltpu.CompilerParams(vmem_limit_bytes=48 * 2**20),
        cost_estimate=pl.CostEstimate(flops=flops, bytes_accessed=16 * 2**20, transcendentals=0),
    )(plan, e_occ, factors, *received, e_own[:, None], e_vir[None, :], *([slabs] * n_steps), density)
    return outs[0], outs[1:]


def decoded(density, plan, entry, skip, codes, count):
    _, vir_own, aux_own = density.shape
    ib = max(1, min(count, 1024 // vir_own))

    def body(plan_ref, code_ref, power_ref, density_ref, out_ref):
        block = pl.program_id(0)
        scales = jnp.exp2(-power_ref[...].astype(jnp.float32)[:, :vir_own])
        for k in range(ib):
            at = lax.broadcasted_iota(jnp.int32, scales.shape, 0) == block * ib + k
            scale = jnp.sum(jnp.where(at, scales, 0.0), axis=0, keepdims=True)
            scale = jnp.broadcast_to(scale, (8, vir_own)).T[:, :1]
            part = code_ref[k * vir_own : (k + 1) * vir_own, :].astype(jnp.float32)
            out_ref[k] = part * scale

    return pl.pallas_call(
        body,
        grid_spec=pltpu.PrefetchScalarGridSpec(
            num_scalar_prefetch=1,
            grid=(count // ib,),
            in_specs=[
                pl.BlockSpec((ib * vir_own, aux_own), lambda i, plan: (i, 0)),
                pl.BlockSpec((TAIL, aux_own), lambda i, plan: (count * vir_own // TAIL, 0)),
                pl.BlockSpec(memory_space=pl.ANY),
            ],
            out_specs=pl.BlockSpec(
                (ib, vir_own, aux_own), lambda i, plan: (plan[entry] // ib + skip // ib + i, 0, 0)
            ),
        ),
        out_shape=jax.ShapeDtypeStruct(density.shape, jnp.float32),
        input_output_aliases={3: 0},
        compiler_params=pltpu.CompilerParams(vmem_limit_bytes=24 * 2**20),
        cost_estimate=pl.CostEstimate(
            flops=0, bytes_accessed=6 * count * vir_own * aux_own, transcendentals=0
        ),
    )(plan, codes, codes, density)


def planned(sizes, factors, e_occ, e_vir, e_own, plan):
    n_occ = lax.axis_size("occ")
    steps = sum(sizes)

    def entry_of(step, partner):
        return step * n_occ + partner

    def row_entry_of(step):
        return steps * n_occ + step

    cuts = 2 if len(sizes) == 1 else 1
    count = IBK // cuts
    starts = [sum(sizes[:u]) for u in range(len(sizes))]
    items = [(u, cut * count) for u in range(len(sizes)) for cut in range(cuts)]
    pair_own = picked(factors, plan, [(row_entry_of(s), 0) for s in range(steps)], 1)
    pair_got = swapped({m: jnp.concatenate(pair_own, axis=0) for m in range(1, n_occ)})
    density = None
    received = []
    for turn, (u, skip) in enumerate(items):
        at = plan if turn == 0 else after(plan, density)
        got = {}
        for partners in rounds_of(n_occ, turn):
            entries = [(entry_of(starts[u], m), skip) for m in partners]
            pieces = dict(zip(partners, picked(factors, at, entries, count)))
            if turn == 0:
                pair_got = after(pair_got, pieces)
            got.update(swapped(pieces))
        received.append([got[m] for m in range(1, n_occ)])
        if turn == 0:
            density = jnp.full(factors.shape, after(jnp.float32(0.0), pair_got[1]), jnp.float32)

    pair_rows = jnp.concatenate(
        [part for s in range(steps) for part in [pair_own[s][0]] + [pair_got[m][s] for m in range(1, n_occ)]],
        axis=1,
    )
    slabs = lax.all_gather(pair_rows, "vir", axis=0, tiled=True)

    coded = []
    for (u, skip), pieces in zip(items, received):
        members = range(starts[u], starts[u] + sizes[u])
        density, codes = pair_block(
            density,
            factors,
            plan,
            e_occ,
            entry_of(starts[u], 0),
            skip,
            [row_entry_of(s) for s in members],
            pieces,
            slabs,
            members,
            e_own,
            e_vir,
        )
        coded.append(codes)

    for turn, ((u, skip), codes) in enumerate(zip(items, coded), len(items)):
        for partners in rounds_of(n_occ, turn):
            got = swapped({m: codes[m - 1] for m in partners})
            for m in partners:
                density = decoded(density, plan, entry_of(starts[u], m), skip, got[m], count)
    return density


def partitions(total, largest):
    if total == 0:
        return [()]
    return [rest + (p,) for p in range(min(total, largest), 0, -1) for rest in partitions(total - p, p)]


def plan_kernel(sizes_list, owned, n_occ, sub_ref, row_ref, plan_ref, branch_ref):
    steps = sub_ref.shape[0]
    subs = [sub_ref[s] for s in range(steps)]

    def total(terms):
        return functools.reduce(lambda a, b: a + b, terms)

    def chosen(holds, value=1):
        return jnp.where(holds, jnp.int32(value), jnp.int32(0))

    shared = [total([chosen(subs[s] == subs[t]) for t in range(steps)]) for s in range(steps)]
    keys = [(shared[s] * (owned // IBK) + subs[s]) * steps + s for s in range(steps)]
    places = [total([chosen(keys[t] < keys[s]) for t in range(steps)]) for s in range(steps)]
    me = lax.axis_index("occ")
    found = []
    for p in range(steps):
        sub = total([chosen(places[s] == p, subs[s]) for s in range(steps)])
        plan_ref[steps * n_occ + p] = total([chosen(places[s] == p, row_ref[s]) for s in range(steps)])
        found.append(total([chosen(places[s] == p, shared[s]) for s in range(steps)]))
        for m in range(n_occ):
            plan_ref[p * n_occ + m] = (me ^ m) * owned + sub * IBK
    branch = jnp.int32(0)
    for b, sizes in enumerate(sizes_list):
        wanted = sum(([p] * p for p in sizes), [])
        missed = total([chosen(have != want) for have, want in zip(found, wanted)])
        branch = jnp.where(missed == 0, jnp.int32(b), branch)
    branch_ref[0] = branch


def shards(factors, e_occ, e_vir, i_sub, j_row):
    vir_own = factors.shape[1]
    n_occ = lax.axis_size("occ")
    owned = factors.shape[0] // n_occ
    steps = i_sub.shape[0]
    sizes_list = [p for p in partitions(steps, steps) if len(p) <= owned // IBK]
    sizes_list.sort(key=lambda sizes: abs(len(sizes) - 2))
    scalars = pl.BlockSpec(memory_space=pltpu.SMEM)
    plan, branch = pl.pallas_call(
        functools.partial(plan_kernel, sizes_list, owned, n_occ),
        in_specs=[scalars, scalars],
        out_specs=[scalars, scalars],
        out_shape=[
            jax.ShapeDtypeStruct((steps * (n_occ + 1),), jnp.int32),
            jax.ShapeDtypeStruct((1,), jnp.int32),
        ],
    )(i_sub, j_row)
    e_own = lax.dynamic_slice_in_dim(e_vir, lax.axis_index("vir") * vir_own, vir_own, 0)
    return lax.switch(
        branch[0],
        [functools.partial(planned, sizes) for sizes in sizes_list],
        factors,
        e_occ,
        e_vir,
        e_own,
        plan,
    )


def solution(mesh):
    placed = (P(None, "vir", "occ"), P(), P(), P(), P())
    return jax.shard_map(
        shards, mesh=mesh, in_specs=placed, out_specs=P(None, "vir", "occ"), check_vma=False
    )
```
